32 devices in a mesh: prow: 16 (over z, y, core), pcol: 2 (over x).
Axes of the slice: x: 2, y: 2, z: 4, core: 2. Of those that a mesh axis runs over, the one named last changes fastest.
Arguments:
- prior_panel: bfloat16 [16384, 12288], P('prow', 'pcol'), may hold values from -0.0546875 to 0.0546875
- prior_solution: bfloat16 [12288, 256], P('pcol', 'prow'), may hold values from -6 to 6
- right_side: bfloat16 [16384, 256], P('prow', 'pcol'), may hold values from -6 to 6
- new_panel: bfloat16 [2, 16384, 512], P(None, 'prow', 'pcol'), may hold values from -0.25 to 0.25
- inverses: bfloat16 [2, 512, 512], P(None, 'pcol'), as said below
Outputs:
- solved: bfloat16 [2, 512, 256], P(None, 'pcol')
- pending: float32 [16384, 256], P('prow', 'pcol')
The draws below stay inside these ranges and needn't reach their ends.
Inputs may be any that keep to these rules, and one draw needn't show every extreme that they name: `inverses`: each of the two inverse blocks is lower triangular with a positive diagonal.
All inputs are finite; a program needn't handle non-finite values.
Results may differ from the reference program's by a relative error of at most 0.0057.
Values may be sent and summed in bfloat16 or wider, within the bound.
A program may use at most 64 MiB of HBM per device.

```python
import math
import jax
import jax.numpy as jnp

NB = 512
RHS = 256
ROWS = 16384
COLS = 12288


def draw_inverses(key, part):
    key_off = jax.random.fold_in(key, 11)
    key_diag = jax.random.fold_in(key, 23)
    spread = 0.7 * jax.random.normal(key_off, (2, NB, NB), jnp.float32)
    lower = jnp.tril(spread, -1) / math.sqrt(NB)
    diag_values = jax.random.uniform(key_diag, (2, NB), jnp.float32, 0.8, 1.6)
    identity = jnp.eye(NB, dtype=jnp.float32)
    return (lower + identity[None, :, :] * diag_values[:, :, None]).astype(jnp.bfloat16)


def spiked(drawn, key, source, target, parts, factor):
    owner, partner = [(jnp.arange(drawn.shape[axis_at]) // (drawn.shape[axis_at] // parts)).reshape([-1 if axis == axis_at else 1 for axis in range(drawn.ndim)]) for axis_at in (source, target)]
    chosen = jax.random.permutation(key, parts)[partner]
    strong = (owner == chosen) | (owner == (partner + parts // 2) % parts)
    return jnp.where(strong, factor * drawn, drawn)


def steps_of(stream_key, shape, shards, low, high):
    loudness, own = 1.0, jax.random.fold_in(stream_key, 6)
    for axis_at, shards_of in shards:
        steps = jnp.exp(jax.random.uniform(jax.random.fold_in(own, axis_at), (shards_of,), jnp.float32, low / len(shards), high / len(shards)))
        loudness = loudness * jnp.repeat(steps, shape[axis_at] // shards_of).reshape([-1 if axis == axis_at else 1 for axis in range(len(shape))])
    return loudness


def scatter_about(stream_key, shape, scale, bound, shards=(), held_as=jnp.bfloat16):
    result = scale * jax.random.normal(stream_key, shape, jnp.float32)
    if shards:
        result = result * steps_of(stream_key, shape, shards, -0.22, 0.18)
    return jnp.clip(result, -bound, bound).astype(held_as)


def bell_draw_with(rng, extent, scale, limit, cuts, heavy, held_as=jnp.bfloat16):
    result = scale * jax.random.normal(rng, extent, jnp.float32)
    if cuts:
        result = result * steps_of(rng, extent, cuts, -0.22, 0.18)
    return jnp.clip(spiked(result, jax.random.fold_in(rng, 3), *heavy), -limit, limit).astype(held_as)


def setup_inputs(seed: int = 0) -> dict:
    key_of = jax.random.split(jax.random.key(seed), 6)
    return {
        "prior_panel": scatter_about(key_of[0], (ROWS, COLS), COLS ** -0.5, 0.0546875, ((0, 16), (1, 2))),
        "prior_solution": bell_draw_with(key_of[1], (COLS, RHS), 1.0, 6.0, ((0, 2), (1, 16)), (0, 1, 16, 2.0)),
        "right_side": scatter_about(key_of[2], (ROWS, RHS), 1.0, 6.0, ((0, 16), (1, 2))),
        "new_panel": scatter_about(key_of[3], (2, ROWS, NB), NB ** -0.5, 0.25, ((1, 16), (2, 2))),
        "inverses": draw_inverses(jax.random.fold_in(key_of[5], 71), 0),
    }


def reference(prior_panel, prior_solution, right_side, new_panel, inverses):
    partial_value = jnp.dot(prior_panel, prior_solution, preferred_element_type=jnp.float32)
    start = right_side.astype(jnp.float32) - partial_value
    row_ids = jnp.arange(ROWS)
    first_panel = jnp.where((row_ids >= NB)[:, None], new_panel[0], jnp.zeros_like(new_panel[0]))
    second_panel = jnp.where((row_ids >= 2 * NB)[:, None], new_panel[1], jnp.zeros_like(new_panel[1]))
    first_block = start[0:NB].astype(jnp.bfloat16)
    first_solved = jnp.dot(inverses[0], first_block, preferred_element_type=jnp.float32).astype(jnp.bfloat16)
    second_rhs = start[NB:2 * NB] - jnp.dot(new_panel[0][NB:2 * NB], first_solved, preferred_element_type=jnp.float32)
    second_block = second_rhs.astype(jnp.bfloat16)
    second_solved = jnp.dot(inverses[1], second_block, preferred_element_type=jnp.float32).astype(jnp.bfloat16)
    pending = start - jnp.dot(first_panel, first_solved, preferred_element_type=jnp.float32)
    pending = pending - jnp.dot(second_panel, second_solved, preferred_element_type=jnp.float32)
    return jnp.stack([first_solved, second_solved]), pending
```

```python
import functools

import jax
import jax.numpy as jnp
from jax import lax
from jax.experimental import pallas as pl
from jax.experimental.pallas import tpu as pltpu
from jax.sharding import PartitionSpec as P

CHUNKS = 8
MESH = pl.DeviceIdType.MESH
F32 = jnp.float32
BF16 = jnp.bfloat16


def kernel(
    R,
    C,
    panel_hbm,
    xt_hbm,
    right_hbm,
    new_hbm,
    inv_hbm,
    solved_ref,
    pending_ref,
    panel,
    xg,
    acc,
    right,
    news,
    invs,
    own,
    out_parts,
    in_parts,
    xs,
    sv,
    panel_sem,
    load_sem,
    ring_send,
    ring_recv,
    sib_send,
    sib_recv,
    news_send,
    news_recv,
    inv_send,
    inv_recv,
    part_send,
    part_recv,
    cast_send,
    cast_recv,
    sv_send,
    sv_recv,
):
    M, K = panel_hbm.shape
    n = R // 2
    Z = n // 2
    H = n // 2
    Q = CHUNKS
    Kc = K // Q
    half = M // 2
    w = right_hbm.shape[1]
    nb = inv_hbm.shape[1]
    C2 = C // 2

    row = lax.axis_index("prow")
    pc = lax.axis_index("pcol")
    core = lax.rem(row, 2)
    chip = row // 2
    y = lax.rem(chip, 2)
    z = chip // 2
    pos = jnp.where(y == 0, z, 2 * Z - 1 - z)

    def chip_at(p):
        p = lax.rem(p + 2 * n, n)
        return jnp.where(p < Z, 2 * p, 2 * (2 * Z - 1 - p) + 1)

    def ring_dev(p):
        return (chip_at(p) * 2 + core, pc)

    rightd, leftd = ring_dev(pos + 1), ring_dev(pos - 1)
    sibd = (chip * 2 + 1 - core, pc)
    others = [lax.rem(pc + d, C) for d in range(1, C)]

    load_x = pltpu.make_async_copy(xt_hbm, xg.at[chip, core], load_sem.at[0])
    load_x.start()
    load_new = pltpu.make_async_copy(new_hbm, news.at[pc], load_sem.at[1])
    load_inv = pltpu.make_async_copy(inv_hbm, invs.at[pc], load_sem.at[2])
    load_right = pltpu.make_async_copy(right_hbm, right, load_sem.at[3])

    def load_panel(k):
        cols = pl.ds(k * Kc, Kc)
        return pltpu.make_async_copy(panel_hbm.at[:, cols], panel.at[:, cols], panel_sem.at[k])

    barrier = pltpu.get_barrier_semaphore()
    peers = [rightd, leftd, sibd] + [(row, t) for t in others]
    for dev in peers:
        pl.semaphore_signal(barrier, inc=1, device_id=dev, device_id_type=MESH)

    for k in range(Q):
        load_panel(k).start()
    load_new.start()
    load_inv.start()
    load_right.start()
    load_x.wait()
    pl.semaphore_wait(barrier, len(peers))

    def hops(direction, k):
        return H if (k + direction) % 2 == 0 else H - 1

    def ring_copy(direction, k, h):
        source = chip_at(pos - h) if direction == 0 else chip_at(pos + h)
        slot = xg.at[source, core, :, pl.ds(k * Kc, Kc)]
        return pltpu.make_async_remote_copy(
            src_ref=slot, dst_ref=slot,
            send_sem=ring_send.at[direction, k, h], recv_sem=ring_recv.at[direction, k, h],
            device_id=rightd if direction == 0 else leftd, device_id_type=MESH)

    def ring_arrival(direction, k, h):
        source = chip_at(pos - h - 1) if direction == 0 else chip_at(pos + h + 1)
        slot = xg.at[source, core, :, pl.ds(k * Kc, Kc)]
        return pltpu.make_async_remote_copy(
            src_ref=slot, dst_ref=slot,
            send_sem=ring_send.at[direction, k, h], recv_sem=ring_recv.at[direction, k, h],
            device_id=rightd if direction == 0 else leftd, device_id_type=MESH)

    def sib_copy(k, mine):
        slot = xg.at[:, core if mine else 1 - core, :, pl.ds(k * Kc, Kc)]
        return pltpu.make_async_remote_copy(
            src_ref=slot, dst_ref=slot, send_sem=sib_send.at[k], recv_sem=sib_recv.at[k],
            device_id=sibd, device_id_type=MESH)

    def send_own(k):
        for direction in range(2):
            if hops(direction, k) > 0:
                ring_copy(direction, k, 0).start()

    new_pieces = [(0, half, half), (0, 0, half), (1, 0, M)]

    def new_copy(t, i, slot):
        s, lo, size = new_pieces[i]
        return pltpu.make_async_remote_copy(
            src_ref=new_hbm.at[s, pl.ds(lo, size)], dst_ref=news.at[slot, s, pl.ds(lo, size)],
            send_sem=news_send.at[t, i], recv_sem=news_recv.at[slot, i],
            device_id=(row, t), device_id_type=MESH)

    def inv_copy(t, slot):
        return pltpu.make_async_remote_copy(
            src_ref=inv_hbm, dst_ref=invs.at[slot],
            send_sem=inv_send.at[t], recv_sem=inv_recv.at[slot],
            device_id=(row, t), device_id_type=MESH)

    send_own(0)
    send_own(1)

    @pl.when(row == 0)
    def _():
        for t in others:
            inv_copy(t, pc).start()

    for t in others:
        new_copy(t, 0, pc).start()

    @pl.when(row > 0)
    def _():
        for t in others:
            new_copy(t, 1, pc).start()
            new_copy(t, 2, pc).start()

    def dot_rows(k, lo, size):
        cols = pl.ds(k * Kc, Kc)
        rows = pl.ds(lo, size)
        x = xg[:, :, :, cols].reshape(w * C, Kc)
        value = lax.dot_general(
            panel[rows, cols], x, (((1,), (1,)), ((), ())), preferred_element_type=F32)
        if k:
            value = acc[rows, :] + value
        return value

    def dot_chunk(k):
        load_panel(k).wait()
        sib_copy(k, False).wait_recv()
        acc[...] = dot_rows(k, 0, M)

    for step in range(1, Q + H):
        for h in range(H, 0, -1):
            k = step - h
            if 0 <= k < Q:
                for direction in range(2):
                    if h - 1 < hops(direction, k):
                        ring_arrival(direction, k, h - 1).wait_recv()
                    if h < hops(direction, k):
                        ring_copy(direction, k, h).start()
                if h == H:
                    sib_copy(k, True).start()
        if 2 <= step + 1 < Q:
            send_own(step + 1)
        if 0 <= step - H - 1 < Q - 1:
            dot_chunk(step - H - 1)

    def part_copy(t, i, slot):
        rows = pl.ds(i * half, half)
        return pltpu.make_async_remote_copy(
            src_ref=out_parts.at[t, rows], dst_ref=in_parts.at[slot, rows],
            send_sem=part_send.at[t, i], recv_sem=part_recv.at[slot, i],
            device_id=(row, t), device_id_type=MESH)

    load_panel(Q - 1).wait()
    sib_copy(Q - 1, False).wait_recv()
    for i in range(2):
        value = dot_rows(Q - 1, i * half, half)
        rows = pl.ds(i * half, half)
        for t in range(C):
            piece = value[:, t * w : (t + 1) * w]
            out_parts[t, rows, :] = piece.astype(BF16)

            @pl.when(pc == t)
            def _():
                own[rows, :] = piece

        for t in others:
            part_copy(t, i, pc).start()

    load_right.wait()
    load_new.wait()
    load_inv.wait()

    def start_rows(i):
        rows = pl.ds(i * half, half)
        value = right[rows, :].astype(F32) - own[rows, :]
        for t in others:
            part_copy(t, i, t).wait_recv()
            value = value - in_parts[t, rows, :].astype(F32)
        return value

    first_half = pl.ds(0, half)
    second_half = pl.ds(half, half)

    def cast_copy(way, s, part):
        slot = xs.at[s, pl.ds(part * C2, C2)]
        return pltpu.make_async_remote_copy(
            src_ref=slot, dst_ref=slot,
            send_sem=cast_send.at[way, s, part], recv_sem=cast_recv.at[s, part],
            device_id=(rightd, leftd, sibd)[way], device_id_type=MESH)

    to_right = (core == 0) & (pos < n // 2)
    to_left = (core == 0) & ((pos == 0) | (pos > n // 2 + 1))
    to_sib = core == 0

    def cast_on(s, part, act):
        for way, flag in enumerate((to_right, to_left, to_sib)):
            @pl.when(flag)
            def _():
                act(cast_copy(way, s, part))

    def sv_copy(t, s, slot):
        return pltpu.make_async_remote_copy(
            src_ref=xs.at[s, t], dst_ref=sv.at[slot, s],
            send_sem=sv_send.at[t, s], recv_sem=sv_recv.at[slot, s],
            device_id=(row, t), device_id_type=MESH)

    def share(s):
        for t in others:
            sv_copy(t, s, pc).start()
        sv[pc, s] = xs[s, pc]

    def product(s, rows):
        total = None
        for c in range(C):
            term = jnp.dot(news[c, s, rows, :], xs[s, c], preferred_element_type=F32)
            total = term if total is None else total + term
        return total

    def solve(s, block):
        for part in range(2):
            for c in range(part * C2, (part + 1) * C2):
                xs[s, c] = jnp.dot(invs[c, s], block, preferred_element_type=F32).astype(BF16)
            cast_on(s, part, lambda copy: copy.start())

    @pl.when(row == 0)
    def _():
        for t in others:
            inv_copy(t, t).wait_recv()
        first = start_rows(0)
        solve(0, first.astype(BF16))
        pending_ref[first_half, :] = first
        for t in others:
            new_copy(t, 0, t).wait_recv()
        second = start_rows(1) - product(0, second_half)
        solve(1, second.astype(BF16))
        pending_ref[second_half, :] = second
        share(0)
        share(1)

    @pl.when(row > 0)
    def _():
        pending_ref[first_half, :] = start_rows(0)
        pending_ref[second_half, :] = start_rows(1)
        for t in others:
            for i in range(3):
                new_copy(t, i, t).wait_recv()
        for s in range(2):
            for part in range(2):
                cast_copy(0, s, part).wait_recv()
                cast_on(s, part, lambda copy: copy.start())
            share(s)
            pending_ref[...] = pending_ref[...] - product(s, pl.ds(0, M))

    for s in range(2):
        for t in others:
            sv_copy(t, s, t).wait_recv()
        solved_ref[s] = jnp.concatenate([sv[c, s] for c in range(C)], axis=1)

    for k in range(Q):
        for direction in range(2):
            for h in range(hops(direction, k)):
                ring_copy(direction, k, h).wait_send()
        sib_copy(k, True).wait_send()
    for t in others:
        new_copy(t, 0, pc).wait_send()
        for i in range(2):
            part_copy(t, i, pc).wait_send()
            sv_copy(t, i, pc).wait_send()

    @pl.when(row == 0)
    def _():
        for t in others:
            inv_copy(t, pc).wait_send()

    @pl.when(row > 0)
    def _():
        for t in others:
            new_copy(t, 1, pc).wait_send()
            new_copy(t, 2, pc).wait_send()

    for s in range(2):
        for part in range(2):
            cast_on(s, part, lambda copy: copy.wait_send())


def body(R, C, prior_panel, prior_solution, right_side, new_panel, inverses):
    M, K = prior_panel.shape
    r = prior_solution.shape[1]
    w = right_side.shape[1]
    nb, NB = inverses.shape[1:]
    assert M == 2 * NB and w * C == r * R and R % 4 == 0 and C % 2 == 0
    Q, H = CHUNKS, R // 4
    dma = pltpu.SemaphoreType.DMA
    any_spec = pl.BlockSpec(memory_space=pl.ANY)
    vmem_spec = pl.BlockSpec(memory_space=pltpu.VMEM)
    return pl.pallas_call(
        functools.partial(kernel, R, C),
        out_shape=(
            jax.ShapeDtypeStruct((2, nb, w * C), BF16),
            jax.ShapeDtypeStruct((M, w), F32),
        ),
        in_specs=[any_spec] * 5,
        out_specs=(vmem_spec, vmem_spec),
        scratch_shapes=[
            pltpu.VMEM((M, K), BF16),
            pltpu.VMEM((R // 2, 2, r, K), BF16),
            pltpu.VMEM((M, w * C), F32),
            pltpu.VMEM((M, w), BF16),
            pltpu.VMEM((C, 2, M, NB // C), BF16),
            pltpu.VMEM((C, 2, nb, NB), BF16),
            pltpu.VMEM((M, w), F32),
            pltpu.VMEM((C, M, w), BF16),
            pltpu.VMEM((C, M, w), BF16),
            pltpu.VMEM((2, C, nb, w), BF16),
            pltpu.VMEM((C, 2, nb, w), BF16),
            dma((Q,)),
            dma((4,)),
            dma((2, Q, H)),
            dma((2, Q, H)),
            dma((Q,)),
            dma((Q,)),
            dma((C, 3)),
            dma((C, 3)),
            dma((C,)),
            dma((C,)),
            dma((C, 2)),
            dma((C, 2)),
            dma((3, 2, 2)),
            dma((2, 2)),
            dma((C, 2)),
            dma((C, 2)),
        ],
        compiler_params=pltpu.CompilerParams(
            collective_id=0, has_side_effects=True, vmem_limit_bytes=50 * 2**20
        ),
    )(prior_panel, prior_solution.T, right_side, new_panel, inverses)


def solution(mesh):
    return jax.shard_map(
        functools.partial(body, mesh.shape["prow"], mesh.shape["pcol"]),
        mesh=mesh,
        in_specs=(
            P("prow", "pcol"),
            P("pcol", "prow"),
            P("prow", "pcol"),
            P(None, "prow", "pcol"),
            P(None, "pcol", None),
        ),
        out_specs=(P(None, "pcol", None), P("prow", "pcol")),
        check_vma=False,
    )
```

```python
import functools

import jax
import jax.numpy as jnp
from jax import lax
from jax.experimental import pallas as pl
from jax.experimental.pallas import tpu as pltpu
from jax.sharding import PartitionSpec as P

CHUNKS = 8
MESH = pl.DeviceIdType.MESH
F32 = jnp.float32
BF16 = jnp.bfloat16


def kernel(
    R,
    C,
    panel_hbm,
    xt_hbm,
    right_hbm,
    new_hbm,
    inv_hbm,
    solved_ref,
    pending_ref,
    panel,
    xg,
    acc,
    right,
    news,
    invs,
    own,
    out_parts,
    in_parts,
    xs,
    sv,
    panel_sem,
    load_sem,
    ring_send,
    ring_recv,
    sib_send,
    sib_recv,
    news_send,
    news_recv,
    inv_send,
    inv_recv,
    part_send,
    part_recv,
    cast_send,
    cast_recv,
    sv_send,
    sv_recv,
):
    M, K = panel_hbm.shape
    n = R // 2
    Z = n // 2
    H = n // 2
    Q = CHUNKS
    Kc = K // Q
    half = M // 2
    w = right_hbm.shape[1]
    nb = inv_hbm.shape[1]
    C2 = C // 2

    row = lax.axis_index("prow")
    pc = lax.axis_index("pcol")
    core = lax.rem(row, 2)
    chip = row // 2
    y = lax.rem(chip, 2)
    z = chip // 2
    pos = jnp.where(y == 0, z, 2 * Z - 1 - z)

    def chip_at(p):
        p = lax.rem(p + 2 * n, n)
        return jnp.where(p < Z, 2 * p, 2 * (2 * Z - 1 - p) + 1)

    def ring_dev(p):
        return (chip_at(p) * 2 + core, pc)

    rightd, leftd = ring_dev(pos + 1), ring_dev(pos - 1)
    sibd = (chip * 2 + 1 - core, pc)
    others = [lax.rem(pc + d, C) for d in range(1, C)]

    load_x = pltpu.make_async_copy(xt_hbm, xg.at[chip, core], load_sem.at[0])
    load_x.start()
    load_new = pltpu.make_async_copy(new_hbm, news.at[pc], load_sem.at[1])
    load_inv = pltpu.make_async_copy(inv_hbm, invs.at[pc], load_sem.at[2])
    load_right = pltpu.make_async_copy(right_hbm, right, load_sem.at[3])

    def load_panel(k):
        cols = pl.ds(k * Kc, Kc)
        return pltpu.make_async_copy(panel_hbm.at[:, cols], panel.at[:, cols], panel_sem.at[k])

    barrier = pltpu.get_barrier_semaphore()
    peers = [rightd, leftd, sibd] + [(row, t) for t in others]
    for dev in peers:
        pl.semaphore_signal(barrier, inc=1, device_id=dev, device_id_type=MESH)

    for k in range(Q):
        load_panel(k).start()
    load_new.start()
    load_inv.start()
    load_right.start()
    load_x.wait()
    pl.semaphore_wait(barrier, len(peers))

    def hops(direction, k):
        return H if (k + direction) % 2 == 0 else H - 1

    def ring_copy(direction, k, h):
        source = chip_at(pos - h) if direction == 0 else chip_at(pos + h)
        slot = xg.at[source, core, :, pl.ds(k * Kc, Kc)]
        return pltpu.make_async_remote_copy(
            src_ref=slot, dst_ref=slot,
            send_sem=ring_send.at[direction, k, h], recv_sem=ring_recv.at[direction, k, h],
            device_id=rightd if direction == 0 else leftd, device_id_type=MESH)

    def ring_arrival(direction, k, h):
        source = chip_at(pos - h - 1) if direction == 0 else chip_at(pos + h + 1)
        slot = xg.at[source, core, :, pl.ds(k * Kc, Kc)]
        return pltpu.make_async_remote_copy(
            src_ref=slot, dst_ref=slot,
            send_sem=ring_send.at[direction, k, h], recv_sem=ring_recv.at[direction, k, h],
            device_id=rightd if direction == 0 else leftd, device_id_type=MESH)

    def sib_copy(k, mine):
        slot = xg.at[:, core if mine else 1 - core, :, pl.ds(k * Kc, Kc)]
        return pltpu.make_async_remote_copy(
            src_ref=slot, dst_ref=slot, send_sem=sib_send.at[k], recv_sem=sib_recv.at[k],
            device_id=sibd, device_id_type=MESH)

    def send_own(k):
        for direction in range(2):
            if hops(direction, k) > 0:
                ring_copy(direction, k, 0).start()

    new_pieces = [(0, half, half), (0, 0, half), (1, 0, M)]

    def new_copy(t, i, slot):
        s, lo, size = new_pieces[i]
        return pltpu.make_async_remote_copy(
            src_ref=new_hbm.at[s, pl.ds(lo, size)], dst_ref=news.at[slot, s, pl.ds(lo, size)],
            send_sem=news_send.at[t, i], recv_sem=news_recv.at[slot, i],
            device_id=(row, t), device_id_type=MESH)

    def inv_copy(t, slot):
        return pltpu.make_async_remote_copy(
            src_ref=inv_hbm, dst_ref=invs.at[slot],
            send_sem=inv_send.at[t], recv_sem=inv_recv.at[slot],
            device_id=(row, t), device_id_type=MESH)

    for k in range(Q):
        send_own(k)

    @pl.when(row == 0)
    def _():
        for t in others:
            inv_copy(t, pc).start()

    for t in others:
        new_copy(t, 0, pc).start()

    @pl.when(row > 0)
    def _():
        for t in others:
            new_copy(t, 1, pc).start()
            new_copy(t, 2, pc).start()

    def dot_rows(k, lo, size):
        cols = pl.ds(k * Kc, Kc)
        rows = pl.ds(lo, size)
        x = xg[:, :, :, cols].reshape(w * C, Kc)
        value = lax.dot_general(
            panel[rows, cols], x, (((1,), (1,)), ((), ())), preferred_element_type=F32)
        if k:
            value = acc[rows, :] + value
        return value

    def dot_chunk(k):
        load_panel(k).wait()
        sib_copy(k, False).wait_recv()
        acc[...] = dot_rows(k, 0, M)

    for h in range(1, H + 1):
        for k in range(Q):
            for direction in range(2):
                if h - 1 < hops(direction, k):
                    ring_arrival(direction, k, h - 1).wait_recv()
                if h < hops(direction, k):
                    ring_copy(direction, k, h).start()
            if h == H:
                sib_copy(k, True).start()
                if k > 0:
                    dot_chunk(k - 1)

    def part_copy(t, i, slot):
        rows = pl.ds(i * half, half)
        return pltpu.make_async_remote_copy(
            src_ref=out_parts.at[t, rows], dst_ref=in_parts.at[slot, rows],
            send_sem=part_send.at[t, i], recv_sem=part_recv.at[slot, i],
            device_id=(row, t), device_id_type=MESH)

    load_panel(Q - 1).wait()
    sib_copy(Q - 1, False).wait_recv()
    for i in range(2):
        value = dot_rows(Q - 1, i * half, half)
        rows = pl.ds(i * half, half)
        for t in range(C):
            piece = value[:, t * w : (t + 1) * w]
            out_parts[t, rows, :] = piece.astype(BF16)

            @pl.when(pc == t)
            def _():
                own[rows, :] = piece

        @pl.when(row != 1)
        def _():
            for t in others:
                part_copy(t, i, pc).start()

    load_right.wait()
    load_new.wait()
    load_inv.wait()

    def start_rows(i):
        rows = pl.ds(i * half, half)
        value = right[rows, :].astype(F32) - own[rows, :]
        for t in others:
            part_copy(t, i, t).wait_recv()
            value = value - in_parts[t, rows, :].astype(F32)
        return value

    first_half = pl.ds(0, half)
    second_half = pl.ds(half, half)

    def cast_copy(way, s, part):
        slot = xs.at[s, pl.ds(part * C2, C2)]
        return pltpu.make_async_remote_copy(
            src_ref=slot, dst_ref=slot,
            send_sem=cast_send.at[way, s, part], recv_sem=cast_recv.at[s, part],
            device_id=(rightd, leftd, sibd)[way], device_id_type=MESH)

    to_right = (core == 0) & (pos < n // 2)
    to_left = (core == 0) & ((pos == 0) | (pos > n // 2 + 1))
    to_sib = core == 0

    def cast_on(s, part, act):
        for way, flag in enumerate((to_right, to_left, to_sib)):
            @pl.when(flag)
            def _():
                act(cast_copy(way, s, part))

    def sv_copy(t, s, slot):
        return pltpu.make_async_remote_copy(
            src_ref=xs.at[s, t], dst_ref=sv.at[slot, s],
            send_sem=sv_send.at[t, s], recv_sem=sv_recv.at[slot, s],
            device_id=(row, t), device_id_type=MESH)

    def share(s):
        for t in others:
            sv_copy(t, s, pc).start()
        sv[pc, s] = xs[s, pc]

    def product(s, rows):
        total = None
        for c in range(C):
            term = jnp.dot(news[c, s, rows, :], xs[s, c], preferred_element_type=F32)
            total = term if total is None else total + term
        return total

    def solve(s, block):
        for part in range(2):
            for c in range(part * C2, (part + 1) * C2):
                xs[s, c] = jnp.dot(invs[c, s], block, preferred_element_type=F32).astype(BF16)
            cast_on(s, part, lambda copy: copy.start())

    @pl.when(row == 0)
    def _():
        for t in others:
            inv_copy(t, t).wait_recv()
        first = start_rows(0)
        solve(0, first.astype(BF16))
        pending_ref[first_half, :] = first
        for t in others:
            new_copy(t, 0, t).wait_recv()
        second = start_rows(1) - product(0, second_half)
        solve(1, second.astype(BF16))
        pending_ref[second_half, :] = second
        share(0)
        share(1)

    @pl.when(row > 0)
    def _():
        for t in others:
            for i in range(3):
                new_copy(t, i, t).wait_recv()
        for part in range(2):
            cast_copy(0, 0, part).wait_recv()
            cast_on(0, part, lambda copy: copy.start())

        @pl.when(row == 1)
        def _():
            for i in range(2):
                for t in others:
                    part_copy(t, i, pc).start()

        share(0)
        acc[:, :w] = product(0, pl.ds(0, M))
        pending_ref[first_half, :] = start_rows(0) - acc[first_half, :w]
        pending_ref[second_half, :] = start_rows(1) - acc[second_half, :w]
        for part in range(2):
            cast_copy(0, 1, part).wait_recv()
            cast_on(1, part, lambda copy: copy.start())
        share(1)
        pending_ref[...] = pending_ref[...] - product(1, pl.ds(0, M))

    for s in range(2):
        for t in others:
            sv_copy(t, s, t).wait_recv()
        solved_ref[s] = jnp.concatenate([sv[c, s] for c in range(C)], axis=1)

    for k in range(Q):
        for direction in range(2):
            for h in range(hops(direction, k)):
                ring_copy(direction, k, h).wait_send()
        sib_copy(k, True).wait_send()
    for t in others:
        new_copy(t, 0, pc).wait_send()
        for i in range(2):
            part_copy(t, i, pc).wait_send()
            sv_copy(t, i, pc).wait_send()

    @pl.when(row == 0)
    def _():
        for t in others:
            inv_copy(t, pc).wait_send()

    @pl.when(row > 0)
    def _():
        for t in others:
            new_copy(t, 1, pc).wait_send()
            new_copy(t, 2, pc).wait_send()

    for s in range(2):
        for part in range(2):
            cast_on(s, part, lambda copy: copy.wait_send())


def body(R, C, prior_panel, prior_solution, right_side, new_panel, inverses):
    M, K = prior_panel.shape
    r = prior_solution.shape[1]
    w = right_side.shape[1]
    nb, NB = inverses.shape[1:]
    assert M == 2 * NB and w * C == r * R and R % 4 == 0 and C % 2 == 0
    Q, H = CHUNKS, R // 4
    dma = pltpu.SemaphoreType.DMA
    any_spec = pl.BlockSpec(memory_space=pltpu.HBM)
    vmem_spec = pl.BlockSpec(memory_space=pltpu.VMEM)
    return pl.pallas_call(
        functools.partial(kernel, R, C),
        out_shape=(
            jax.ShapeDtypeStruct((2, nb, w * C), BF16),
            jax.ShapeDtypeStruct((M, w), F32),
        ),
        in_specs=[any_spec] * 5,
        out_specs=(vmem_spec, vmem_spec),
        scratch_shapes=[
            pltpu.VMEM((M, K), BF16),
            pltpu.VMEM((R // 2, 2, r, K), BF16),
            pltpu.VMEM((M, w * C), F32),
            pltpu.VMEM((M, w), BF16),
            pltpu.VMEM((C, 2, M, NB // C), BF16),
            pltpu.VMEM((C, 2, nb, NB), BF16),
            pltpu.VMEM((M, w), F32),
            pltpu.VMEM((C, M, w), BF16),
            pltpu.VMEM((C, M, w), BF16),
            pltpu.VMEM((2, C, nb, w), BF16),
            pltpu.VMEM((C, 2, nb, w), BF16),
            dma((Q,)),
            dma((4,)),
            dma((2, Q, H)),
            dma((2, Q, H)),
            dma((Q,)),
            dma((Q,)),
            dma((C, 3)),
            dma((C, 3)),
            dma((C,)),
            dma((C,)),
            dma((C, 2)),
            dma((C, 2)),
            dma((3, 2, 2)),
            dma((2, 2)),
            dma((C, 2)),
            dma((C, 2)),
        ],
        compiler_params=pltpu.CompilerParams(
            collective_id=0, has_side_effects=True, vmem_limit_bytes=62 * 2**20
        ),
    )(prior_panel, prior_solution.T, right_side, new_panel, inverses)


def solution(mesh):
    return jax.shard_map(
        functools.partial(body, mesh.shape["prow"], mesh.shape["pcol"]),
        mesh=mesh,
        in_specs=(
            P("prow", "pcol"),
            P("pcol", "prow"),
            P("prow", "pcol"),
            P(None, "prow", "pcol"),
            P(None, "pcol", None),
        ),
        out_specs=(P(None, "pcol", None), P("prow", "pcol")),
        check_vma=False,
    )
```

```python
import functools

import jax
import jax.numpy as jnp
from jax import lax
from jax.experimental import pallas as pl
from jax.experimental.pallas import tpu as pltpu
from jax.sharding import PartitionSpec as P

CHUNKS = 3
MESH = pl.DeviceIdType.MESH
F32 = jnp.float32
BF16 = jnp.bfloat16


def kernel(
    R,
    C,
    panel_hbm,
    xt_hbm,
    right_hbm,
    new_hbm,
    inv_hbm,
    solved_ref,
    pending_ref,
    panel,
    xg,
    acc,
    right,
    news,
    invs,
    own,
    out_parts,
    in_parts,
    xs,
    sv,
    panel_sem,
    load_sem,
    ring_send,
    ring_recv,
    sib_send,
    sib_recv,
    news_send,
    news_recv,
    inv_send,
    inv_recv,
    part_send,
    part_recv,
    cast_send,
    cast_recv,
    sv_send,
    sv_recv,
):
    M, K = panel_hbm.shape
    n = R // 2
    Z = n // 2
    H = n // 2
    Q = CHUNKS
    Kc = K // Q
    half = M // 2
    w = right_hbm.shape[1]
    nb = inv_hbm.shape[1]
    C2 = C // 2

    row = lax.axis_index("prow")
    pc = lax.axis_index("pcol")
    core = lax.rem(row, 2)
    chip = row // 2
    y = lax.rem(chip, 2)
    z = chip // 2
    pos = jnp.where(y == 0, z, 2 * Z - 1 - z)

    def chip_at(p):
        p = lax.rem(p + 2 * n, n)
        return jnp.where(p < Z, 2 * p, 2 * (2 * Z - 1 - p) + 1)

    def ring_dev(p):
        return (chip_at(p) * 2 + core, pc)

    rightd, leftd = ring_dev(pos + 1), ring_dev(pos - 1)
    sibd = (chip * 2 + 1 - core, pc)
    others = [lax.rem(pc + d, C) for d in range(1, C)]

    load_x = pltpu.make_async_copy(xt_hbm, xg.at[chip, core], load_sem.at[0])
    load_x.start()
    load_new = pltpu.make_async_copy(new_hbm, news.at[pc], load_sem.at[1])
    load_inv = pltpu.make_async_copy(inv_hbm, invs.at[pc], load_sem.at[2])
    load_right = pltpu.make_async_copy(right_hbm, right, load_sem.at[3])

    def load_panel(k):
        cols = pl.ds(k * Kc, Kc)
        return pltpu.make_async_copy(panel_hbm.at[:, cols], panel.at[:, cols], panel_sem.at[k])

    barrier = pltpu.get_barrier_semaphore()
    peers = [rightd, leftd, sibd] + [(row, t) for t in others]
    for dev in peers:
        pl.semaphore_signal(barrier, inc=1, device_id=dev, device_id_type=MESH)

    for k in range(Q):
        load_panel(k).start()
    load_new.start()
    load_inv.start()
    load_right.start()
    load_x.wait()
    pl.semaphore_wait(barrier, len(peers))

    def hops(direction, k):
        return H if (k + direction) % 2 == 0 else H - 1

    def ring_copy(direction, k, h):
        source = chip_at(pos - h) if direction == 0 else chip_at(pos + h)
        slot = xg.at[source, core, :, pl.ds(k * Kc, Kc)]
        return pltpu.make_async_remote_copy(
            src_ref=slot, dst_ref=slot,
            send_sem=ring_send.at[direction, k, h], recv_sem=ring_recv.at[direction, k, h],
            device_id=rightd if direction == 0 else leftd, device_id_type=MESH)

    def ring_arrival(direction, k, h):
        source = chip_at(pos - h - 1) if direction == 0 else chip_at(pos + h + 1)
        slot = xg.at[source, core, :, pl.ds(k * Kc, Kc)]
        return pltpu.make_async_remote_copy(
            src_ref=slot, dst_ref=slot,
            send_sem=ring_send.at[direction, k, h], recv_sem=ring_recv.at[direction, k, h],
            device_id=rightd if direction == 0 else leftd, device_id_type=MESH)

    def sib_copy(k, mine):
        slot = xg.at[:, core if mine else 1 - core, :, pl.ds(k * Kc, Kc)]
        return pltpu.make_async_remote_copy(
            src_ref=slot, dst_ref=slot, send_sem=sib_send.at[k], recv_sem=sib_recv.at[k],
            device_id=sibd, device_id_type=MESH)

    def send_own(k):
        for direction in range(2):
            if hops(direction, k) > 0:
                ring_copy(direction, k, 0).start()

    new_pieces = [(0, half, half), (0, 0, half), (1, 0, M)]

    def new_copy(t, i, slot):
        s, lo, size = new_pieces[i]
        return pltpu.make_async_remote_copy(
            src_ref=new_hbm.at[s, pl.ds(lo, size)], dst_ref=news.at[slot, s, pl.ds(lo, size)],
            send_sem=news_send.at[t, i], recv_sem=news_recv.at[slot, i],
            device_id=(row, t), device_id_type=MESH)

    def inv_copy(t, slot):
        return pltpu.make_async_remote_copy(
            src_ref=inv_hbm, dst_ref=invs.at[slot],
            send_sem=inv_send.at[t], recv_sem=inv_recv.at[slot],
            device_id=(row, t), device_id_type=MESH)

    for k in range(Q):
        send_own(k)

    @pl.when(row == 0)
    def _():
        for t in others:
            inv_copy(t, pc).start()

    for t in others:
        new_copy(t, 0, pc).start()

    @pl.when(row > 0)
    def _():
        for t in others:
            new_copy(t, 1, pc).start()
            new_copy(t, 2, pc).start()

    def dot_rows(k, lo, size):
        cols = pl.ds(k * Kc, Kc)
        rows = pl.ds(lo, size)
        x = xg[:, :, :, cols].reshape(w * C, Kc)
        value = lax.dot_general(
            panel[rows, cols], x, (((1,), (1,)), ((), ())), preferred_element_type=F32)
        if k:
            value = acc[rows, :] + value
        return value

    def dot_chunk(k):
        load_panel(k).wait()
        sib_copy(k, False).wait_recv()
        acc[...] = dot_rows(k, 0, M)

    for h in range(1, H + 1):
        for k in range(Q):
            for direction in range(2):
                if h - 1 < hops(direction, k):
                    ring_arrival(direction, k, h - 1).wait_recv()
                if h < hops(direction, k):
                    ring_copy(direction, k, h).start()
            if h == H:
                sib_copy(k, True).start()
                if k > 0:
                    dot_chunk(k - 1)

    def part_copy(t, i, slot):
        rows = pl.ds(i * half, half)
        return pltpu.make_async_remote_copy(
            src_ref=out_parts.at[t, rows], dst_ref=in_parts.at[slot, rows],
            send_sem=part_send.at[t, i], recv_sem=part_recv.at[slot, i],
            device_id=(row, t), device_id_type=MESH)

    load_panel(Q - 1).wait()
    sib_copy(Q - 1, False).wait_recv()
    for i in range(2):
        value = dot_rows(Q - 1, i * half, half)
        rows = pl.ds(i * half, half)
        for t in range(C):
            piece = value[:, t * w : (t + 1) * w]
            out_parts[t, rows, :] = piece.astype(BF16)

            @pl.when(pc == t)
            def _():
                own[rows, :] = piece

        @pl.when(row != 1)
        def _():
            for t in others:
                part_copy(t, i, pc).start()

    load_right.wait()
    load_new.wait()
    load_inv.wait()

    def start_rows(i):
        rows = pl.ds(i * half, half)
        value = right[rows, :].astype(F32) - own[rows, :]
        for t in others:
            part_copy(t, i, t).wait_recv()
            value = value - in_parts[t, rows, :].astype(F32)
        return value

    first_half = pl.ds(0, half)
    second_half = pl.ds(half, half)

    def cast_copy(way, s, part):
        slot = xs.at[s, pl.ds(part * C2, C2)]
        return pltpu.make_async_remote_copy(
            src_ref=slot, dst_ref=slot,
            send_sem=cast_send.at[way, s, part], recv_sem=cast_recv.at[s, part],
            device_id=(rightd, leftd, sibd)[way], device_id_type=MESH)

    to_right = (core == 0) & (pos < n // 2)
    to_left = (core == 0) & ((pos == 0) | (pos > n // 2 + 1))
    to_sib = core == 0

    def cast_on(s, part, act):
        for way, flag in enumerate((to_right, to_left, to_sib)):
            @pl.when(flag)
            def _():
                act(cast_copy(way, s, part))

    def sv_copy(t, s, slot):
        return pltpu.make_async_remote_copy(
            src_ref=xs.at[s, t], dst_ref=sv.at[slot, s],
            send_sem=sv_send.at[t, s], recv_sem=sv_recv.at[slot, s],
            device_id=(row, t), device_id_type=MESH)

    def share(s):
        for t in others:
            sv_copy(t, s, pc).start()
        sv[pc, s] = xs[s, pc]

    def product(s, rows):
        total = None
        for c in range(C):
            term = jnp.dot(news[c, s, rows, :], xs[s, c], preferred_element_type=F32)
            total = term if total is None else total + term
        return total

    def solve(s, block):
        for part in range(2):
            for c in range(part * C2, (part + 1) * C2):
                xs[s, c] = jnp.dot(invs[c, s], block, preferred_element_type=F32).astype(BF16)
            cast_on(s, part, lambda copy: copy.start())

    @pl.when(row == 0)
    def _():
        for t in others:
            inv_copy(t, t).wait_recv()
        first = start_rows(0)
        solve(0, first.astype(BF16))
        pending_ref[first_half, :] = first
        for t in others:
            new_copy(t, 0, t).wait_recv()
        second = start_rows(1) - product(0, second_half)
        solve(1, second.astype(BF16))
        pending_ref[second_half, :] = second
        share(0)
        share(1)

    @pl.when(row > 0)
    def _():
        for t in others:
            for i in range(3):
                new_copy(t, i, t).wait_recv()
        for part in range(2):
            cast_copy(0, 0, part).wait_recv()
            cast_on(0, part, lambda copy: copy.start())

        @pl.when(row == 1)
        def _():
            for i in range(2):
                for t in others:
                    part_copy(t, i, pc).start()

        share(0)
        acc[:, :w] = product(0, pl.ds(0, M))
        pending_ref[first_half, :] = start_rows(0) - acc[first_half, :w]
        pending_ref[second_half, :] = start_rows(1) - acc[second_half, :w]
        for part in range(2):
            cast_copy(0, 1, part).wait_recv()
            cast_on(1, part, lambda copy: copy.start())
        share(1)
        pending_ref[...] = pending_ref[...] - product(1, pl.ds(0, M))

    for s in range(2):
        for t in others:
            sv_copy(t, s, t).wait_recv()
        solved_ref[s] = jnp.concatenate([sv[c, s] for c in range(C)], axis=1)

    for k in range(Q):
        for direction in range(2):
            for h in range(hops(direction, k)):
                ring_copy(direction, k, h).wait_send()
        sib_copy(k, True).wait_send()
    for t in others:
        new_copy(t, 0, pc).wait_send()
        for i in range(2):
            part_copy(t, i, pc).wait_send()
            sv_copy(t, i, pc).wait_send()

    @pl.when(row == 0)
    def _():
        for t in others:
            inv_copy(t, pc).wait_send()

    @pl.when(row > 0)
    def _():
        for t in others:
            new_copy(t, 1, pc).wait_send()
            new_copy(t, 2, pc).wait_send()

    for s in range(2):
        for part in range(2):
            cast_on(s, part, lambda copy: copy.wait_send())


def body(R, C, prior_panel, prior_solution, right_side, new_panel, inverses):
    M, K = prior_panel.shape
    r = prior_solution.shape[1]
    w = right_side.shape[1]
    nb, NB = inverses.shape[1:]
    assert M == 2 * NB and w * C == r * R and R % 4 == 0 and C % 2 == 0
    Q, H = CHUNKS, R // 4
    dma = pltpu.SemaphoreType.DMA
    any_spec = pl.BlockSpec(memory_space=pltpu.HBM)
    vmem_spec = pl.BlockSpec(memory_space=pltpu.VMEM)
    return pl.pallas_call(
        functools.partial(kernel, R, C),
        out_shape=(
            jax.ShapeDtypeStruct((2, nb, w * C), BF16),
            jax.ShapeDtypeStruct((M, w), F32),
        ),
        in_specs=[any_spec] * 5,
        out_specs=(vmem_spec, vmem_spec),
        scratch_shapes=[
            pltpu.VMEM((M, K), BF16),
            pltpu.VMEM((R // 2, 2, r, K), BF16),
            pltpu.VMEM((M, w * C), F32),
            pltpu.VMEM((M, w), BF16),
            pltpu.VMEM((C, 2, M, NB // C), BF16),
            pltpu.VMEM((C, 2, nb, NB), BF16),
            pltpu.VMEM((M, w), F32),
            pltpu.VMEM((C, M, w), BF16),
            pltpu.VMEM((C, M, w), BF16),
            pltpu.VMEM((2, C, nb, w), BF16),
            pltpu.VMEM((C, 2, nb, w), BF16),
            dma((Q,)),
            dma((4,)),
            dma((2, Q, H)),
            dma((2, Q, H)),
            dma((Q,)),
            dma((Q,)),
            dma((C, 3)),
            dma((C, 3)),
            dma((C,)),
            dma((C,)),
            dma((C, 2)),
            dma((C, 2)),
            dma((3, 2, 2)),
            dma((2, 2)),
            dma((C, 2)),
            dma((C, 2)),
        ],
        compiler_params=pltpu.CompilerParams(
            collective_id=0, has_side_effects=True, vmem_limit_bytes=62 * 2**20
        ),
    )(prior_panel, prior_solution.T, right_side, new_panel, inverses)


def solution(mesh):
    return jax.shard_map(
        functools.partial(body, mesh.shape["prow"], mesh.shape["pcol"]),
        mesh=mesh,
        in_specs=(
            P("prow", "pcol"),
            P("pcol", "prow"),
            P("prow", "pcol"),
            P(None, "prow", "pcol"),
            P(None, "pcol", None),
        ),
        out_specs=(P(None, "pcol", None), P("prow", "pcol")),
        check_vma=False,
    )
```
